128 devices in a mesh: row: 16 (over y, z), col: 8 (over x, core).
Axes of the slice: x: 4, y: 4, z: 4, core: 2. Of those that a mesh axis runs over, the one named last changes fastest.
Arguments:
- panel_t: float32 [64, 16384], P(None, ('row', 'col')), may hold values from -0.1875 to 0.1875
- panel_grad_t: float32 [64, 16384], P(None, ('row', 'col')), may hold values from -1.2 to 1.2
- diag_factor: float32 [64, 64], replicated, may hold values from -0.1 to 2, as said below
- diag_grad: float32 [64, 64], replicated, may hold values from -3 to 3, as said below
- row_panel: float32 [64, 16384], P('row', 'col'), may hold values from -3 to 3
- row_grad: float32 [64, 16384], P('row', 'col'), may hold values from -3 to 3
- trailing: float32 [16384, 16384], P('row', 'col'), may hold values from -0.1875 to 0.1875
- trailing_grad: float32 [16384, 16384], P('row', 'col'), may hold values from -6 to 6
Outputs:
- panel_out: float32 [64, 16384], P(None, ('row', 'col'))
- trailing_out: float32 [16384, 16384], P('row', 'col')
- row_out: float32 [64, 16384], P('row', 'col')
- diag_out: float32 [64, 64], replicated
The draws below stay inside these ranges and needn't reach their ends.
Inputs may be any that keep to these rules, and one draw needn't show every extreme that they name: `diag_factor`: lower triangular; diagonal between 1 and 2, entries below it within 0.1 in magnitude. `diag_grad`: lower triangular.
All inputs are finite; a program needn't handle non-finite values.
Results may differ from the reference program's by a relative error of at most 0.000078.
Values sent between devices are 32-bit elements; how exact they have to be, the bound alone decides.
No kernel may reach another device: no remote copies, remote signals or barrier semaphores. Data moves between devices by JAX's collectives and lax.ppermute only.
A program may use at most 64 MiB of HBM per device.

```python
import jax
import jax.numpy as jnp
from jax import lax

PANEL = 64
ROWS = 16384
COLS = 16384


def draw_diag_factor(key, part):
    key = jax.random.fold_in(key, 11)
    first, second = jax.random.split(key)
    middle = jax.random.uniform(first, (PANEL,), jnp.float32, 1.0, 2.0)
    below = jax.random.uniform(second, (PANEL, PANEL), jnp.float32, -0.1, 0.1)
    return jnp.tril(below, -1) + jnp.diag(middle)


def draw_diag_grad(key, part):
    key = jax.random.fold_in(key, 23)
    values = 0.5 * jax.random.truncated_normal(key, -6.0, 6.0, (PANEL, PANEL), jnp.float32)
    return jnp.tril(values)


def levels(stream_key, dims, shards, least, largest):
    factor_of = 1.0
    for position, parts in shards:
        draws = jax.random.uniform(jax.random.fold_in(jax.random.fold_in(stream_key, 6), position), (parts,), jnp.float32, least / len(shards), largest / len(shards))
        factor_of = factor_of * jnp.repeat(jnp.exp(draws), dims[position] // parts).reshape((-1,) + (1,) * (len(dims) - 1 - position))
    return factor_of


def gaussian(rng, extent, width, bound, cuts=(), held_as=jnp.bfloat16):
    drawn = jax.random.normal(rng, extent, jnp.float32) * width
    if len(cuts) > 0:
        drawn = levels(rng, extent, cuts, -0.22, 0.18) * drawn
    return jnp.clip(drawn, min=-bound, max=bound).astype(held_as)


def setup_inputs(seed: int = 0) -> dict:
    splits = jax.random.split(jax.random.key(seed), 9)
    panel_t = gaussian(splits[0], (PANEL, ROWS), (ROWS // 16) ** -0.5, 0.1875, ((1, 128),), jnp.float32)
    panel_grad_t = gaussian(splits[1], (PANEL, ROWS), 0.2, 1.2, ((1, 128),), jnp.float32)
    diag_factor = draw_diag_factor(jax.random.fold_in(splits[8], 71), 0)
    diag_grad = draw_diag_grad(jax.random.fold_in(splits[8], 71), 0)
    row_panel = gaussian(splits[4], (PANEL, COLS), 0.5, 3.0, ((0, 16), (1, 8)), jnp.float32)
    row_grad = gaussian(splits[5], (PANEL, COLS), 0.5, 3.0, ((0, 16), (1, 8)), jnp.float32)
    trailing = gaussian(splits[6], (ROWS, COLS), (ROWS // 16) ** -0.5, 0.1875, ((0, 16), (1, 8)), jnp.float32)
    trailing_grad = gaussian(splits[7], (ROWS, COLS), 1.0, 6.0, ((0, 16), (1, 8)), jnp.float32)
    return {"panel_t": panel_t, "panel_grad_t": panel_grad_t, "diag_factor": diag_factor, "diag_grad": diag_grad, "row_panel": row_panel, "row_grad": row_grad, "trailing": trailing, "trailing_grad": trailing_grad}


def solve_transposed(factor, values):
    return lax.linalg.triangular_solve(factor, values, left_side=True, lower=True, transpose_a=True)

def reference(panel_t, panel_grad_t, diag_factor, diag_grad, row_panel, row_grad, trailing, trailing_grad):
    highest = lax.Precision.HIGHEST
    panel_out = solve_transposed(diag_factor, panel_grad_t)
    trailing_out = trailing_grad - jnp.dot(panel_out.T, row_panel, precision=highest)
    dsum = diag_grad - jnp.tril(jnp.dot(panel_out, panel_t.T, precision=highest))
    phi = jnp.tril(jnp.dot(diag_factor.T, dsum, precision=highest))
    phi = phi - 0.5 * jnp.diag(jnp.diag(phi))
    inner = solve_transposed(diag_factor, phi)
    spart = lax.linalg.triangular_solve(diag_factor, inner, left_side=False, lower=True, transpose_a=False)
    both = spart + spart.T
    diag_out = 0.5 * both
    row_out = row_grad - jnp.dot(panel_out, trailing, precision=highest) - jnp.dot(both, row_panel, precision=highest)
    return (panel_out, trailing_out, row_out, diag_out)
```

```python
import jax
import jax.numpy as jnp
from jax import lax
from jax.experimental import pallas as pl
from jax.experimental.pallas import tpu as pltpu
from jax.sharding import PartitionSpec as P

N = 64
ROWS = 16
COLS = 8
LOCAL = 128
TILE_ROWS = COLS * LOCAL
TILE_COLS = 2048
OWN = N // ROWS
PIECES = TILE_COLS // 128
HIGHEST = lax.Precision.HIGHEST
F32 = jnp.float32
BF16 = jnp.bfloat16
MIB = 1024 * 1024


def dot(a, b, contract, precision=None):
    return lax.dot_general(
        a, b, ((contract[:1], contract[1:]), ((), ())), precision=precision, preferred_element_type=F32
    )


def split(value):
    high = value.astype(BF16)
    return high, (value - high.astype(F32)).astype(BF16)


def payload_kernel(grad_ref, panel_ref, out_ref):
    grad = grad_ref[...]
    term = dot(grad, panel_ref[...], (1, 1), HIGHEST)
    out_ref[:N, :] = grad
    out_ref[N:, :N] = term[: N // 2]
    out_ref[N:, N:] = term[N // 2 :]


def inverse_kernel(factor_ref, out_ref):
    factor = factor_ref[...]
    row = lax.broadcasted_iota(jnp.int32, (N, N), 0)
    col = lax.broadcasted_iota(jnp.int32, (N, N), 1)
    eye = jnp.where(row == col, 1.0, 0.0).astype(F32)
    diagonal = jnp.sum(factor * eye, axis=1, keepdims=True)
    diagonal_row = jnp.sum(factor * eye, axis=0, keepdims=True)
    below = jnp.where(row > col, factor, 0.0) / diagonal
    value = eye
    for j in range(N - 1):
        value = value - below[:, j : j + 1] * value[j : j + 1, :]
    out_ref[...] = value / diagonal_row


def product_kernel(
    near_ref, far_ref, inverse_ref, row_panel_ref, trailing_ref,
    own_ref, left_ref, send_ref,
    tile, gathered, rows, sems,
):
    chunk = 256
    copies = []
    for i in range(TILE_COLS // chunk):
        cols = pl.ds(i * chunk, chunk)
        copies.append(pltpu.make_async_copy(trailing_ref.at[:, cols], tile.at[:, cols], sems.at[i]))
        copies[-1].start()
    place = lax.axis_index("col")
    chip, core = place // 2, lax.rem(place, 2)
    for k in range(4):
        from_chip = lax.rem(chip - k + 4, 4) * 2
        for ref, which in ((near_ref, core), (far_ref, 1 - core)):
            start = pl.multiple_of((from_chip + which) * LOCAL, LOCAL)
            gathered[:, pl.ds(start, LOCAL)] = ref[k, :N, :]
    term = near_ref[0, N:, :] + far_ref[0, N:, :]
    for k in range(1, 4):
        term = term + near_ref[k, N:, :] + far_ref[k, N:, :]
    for j in range(PIECES):
        rows[OWN * j : OWN * (j + 1), :] = row_panel_ref[:, 128 * j : 128 * (j + 1)]
    own_rows = rows[...]
    for s in range(ROWS):
        send_ref[s, N : 2 * N, :] = own_rows
        send_ref[s, 2 * N :, :] = term
    solved = dot(inverse_ref[...], gathered[...], (0, 0), HIGHEST)
    gathered[...] = solved
    own_ref[...] = gathered[:, pl.ds(pl.multiple_of(place * LOCAL, LOCAL), LOCAL)]
    high, low = split(solved)
    both = jnp.concatenate([high, low], axis=0)
    doubled = jnp.concatenate([solved, solved], axis=0).T
    lane = lax.broadcasted_iota(jnp.int32, doubled.shape, 1)
    rounded = doubled.astype(BF16).astype(F32)
    pieces = jnp.where(lane < N, rounded, doubled - rounded).astype(BF16)
    left_ref[:, : 2 * N] = pieces
    left_ref[:, 2 * N :] = pieces
    for i in range(TILE_COLS // chunk):
        copies[i].wait()
        t_high, t_low = split(tile[:, i * chunk : (i + 1) * chunk])
        part = dot(both, t_high, (1, 0)) + dot(both, t_low, (1, 0))
        part = part[:N] + part[N:]
        for s in range(ROWS):
            for jj in range(chunk // 128):
                j = i * (chunk // 128) + jj
                send_ref[s, OWN * j : OWN * (j + 1), :] = part[OWN * s : OWN * (s + 1), 128 * jj : 128 * (jj + 1)]


def update_kernel(
    recv_ref, left_ref, inverse_ref, factor_ref, diag_grad_ref, row_grad_ref, grad_ref,
    out_ref, row_out_ref, diag_out_ref,
    grad, result, full, right, small, in_sems, out_sems,
):
    count = 8
    height = TILE_ROWS // count
    loads, stores = [], []
    for i in range(count):
        part = pl.ds(i * height, height)
        loads.append(pltpu.make_async_copy(grad_ref.at[part], grad.at[part], in_sems.at[i]))
        stores.append(pltpu.make_async_copy(result.at[part], out_ref.at[part], out_sems.at[i]))
        loads[-1].start()
    for s in range(ROWS):
        for j in range(PIECES):
            full[OWN * s : OWN * (s + 1), 128 * j : 128 * (j + 1)] = recv_ref[s, N + OWN * j : N + OWN * (j + 1), :]
    high, low = split(full[...])
    right[:N] = high
    right[N : 2 * N] = high
    right[2 * N : 3 * N] = low
    right[3 * N :] = low

    def step(i):
        loads[i].wait()
        part = slice(i * height, (i + 1) * height)
        result[part] = grad[part] - dot(left_ref[part], right[...], (1, 0))
        stores[i].start()

    for i in range(count // 2):
        step(i)

    packed = recv_ref[0, 2 * N :, :]
    reduced = recv_ref[0, :N, :]
    for s in range(1, ROWS):
        packed = packed + recv_ref[s, 2 * N :, :]
        reduced = reduced + recv_ref[s, :N, :]
    total = jnp.concatenate([packed[:, :N], packed[:, N:]], axis=0)
    inverse, factor = inverse_ref[...], factor_ref[...]
    r_id = lax.broadcasted_iota(jnp.int32, (N, N), 0)
    c_id = lax.broadcasted_iota(jnp.int32, (N, N), 1)
    lower = r_id >= c_id
    dsum = diag_grad_ref[...] - jnp.where(lower, dot(inverse, total, (0, 0), HIGHEST), 0.0)
    phi = jnp.where(lower, dot(factor, dsum, (0, 0), HIGHEST), 0.0)
    phi = jnp.where(r_id == c_id, 0.5 * phi, phi)
    spart = dot(dot(inverse, phi, (0, 0), HIGHEST), inverse, (1, 0), HIGHEST)
    both = spart + spart.T
    diag_out_ref[...] = 0.5 * both
    small[...] = both
    own_both = small[pl.ds(lax.axis_index("row") * OWN, OWN), :]
    both_high, both_low = split(own_both)
    wide = jnp.concatenate([both_high, both_low, both_high, both_low], axis=1)
    second = dot(wide, right[...], (1, 0))
    for j in range(PIECES):
        cols = slice(128 * j, 128 * (j + 1))
        row_out_ref[:, cols] = row_grad_ref[:, cols] - reduced[OWN * j : OWN * (j + 1), :] - second[:, cols]

    for i in range(count // 2, count):
        step(i)
    for copy in stores:
        copy.wait()


def across_chips(value, k):
    pairs = [(2 * x + c, 2 * ((x + k) % 4) + c) for x in range(4) for c in range(2)]
    return lax.ppermute(value, "col", pairs)


def per_device(panel_t, panel_grad_t, diag_factor, diag_grad, row_panel, row_grad, trailing, trailing_grad):
    vmem = pl.BlockSpec(memory_space=pltpu.VMEM)
    anywhere = pl.BlockSpec(memory_space=pl.ANY)
    payload = pl.pallas_call(
        payload_kernel,
        out_shape=jax.ShapeDtypeStruct((N + N // 2, LOCAL), F32),
        in_specs=[vmem, vmem],
        out_specs=vmem,
        name="payload",
    )(panel_grad_t, panel_t)
    opposite = across_chips(payload, 2)
    right = across_chips(payload, 1)
    left = across_chips(payload, 3)
    inverse = pl.pallas_call(
        inverse_kernel,
        out_shape=jax.ShapeDtypeStruct((N, N), F32),
        in_specs=[vmem],
        out_specs=vmem,
        name="inverse",
    )(diag_factor)
    near = jnp.stack([payload, right, opposite, left])
    far = lax.ppermute(near, "col", [(i, i ^ 1) for i in range(COLS)])
    panel_out, left_factor, send = pl.pallas_call(
        product_kernel,
        out_shape=(
            jax.ShapeDtypeStruct((N, LOCAL), F32),
            jax.ShapeDtypeStruct((TILE_ROWS, 4 * N), BF16),
            jax.ShapeDtypeStruct((ROWS, 2 * N + N // 2, 128), F32),
        ),
        in_specs=[vmem] * 4 + [anywhere],
        out_specs=(vmem,) * 3,
        scratch_shapes=[
            pltpu.VMEM((TILE_ROWS, TILE_COLS), F32),
            pltpu.VMEM((N, TILE_ROWS), F32),
            pltpu.VMEM((N, 128), F32),
            pltpu.SemaphoreType.DMA((8,)),
        ],
        compiler_params=pltpu.CompilerParams(vmem_limit_bytes=24 * MIB),
        name="product",
    )(near, far, inverse, row_panel, trailing)
    recv = lax.all_to_all(send, "row", 0, 0)
    trailing_out, row_out, diag_out = pl.pallas_call(
        update_kernel,
        out_shape=(
            jax.ShapeDtypeStruct((TILE_ROWS, TILE_COLS), F32),
            jax.ShapeDtypeStruct((OWN, TILE_COLS), F32),
            jax.ShapeDtypeStruct((N, N), F32),
        ),
        in_specs=[vmem] * 6 + [anywhere],
        out_specs=(anywhere, vmem, vmem),
        scratch_shapes=[
            pltpu.VMEM((TILE_ROWS, TILE_COLS), F32),
            pltpu.VMEM((TILE_ROWS, TILE_COLS), F32),
            pltpu.VMEM((N, TILE_COLS), F32),
            pltpu.VMEM((4 * N, TILE_COLS), BF16),
            pltpu.VMEM((N, N), F32),
            pltpu.SemaphoreType.DMA((8,)),
            pltpu.SemaphoreType.DMA((8,)),
        ],
        compiler_params=pltpu.CompilerParams(vmem_limit_bytes=32 * MIB),
        name="update",
    )(recv, left_factor, inverse, diag_factor, diag_grad, row_grad, trailing_grad)
    return (panel_out, trailing_out, row_out, diag_out)


def solution(mesh):
    return jax.shard_map(
        per_device,
        mesh=mesh,
        in_specs=(
            P(None, ("row", "col")),
            P(None, ("row", "col")),
            P(),
            P(),
            P("row", "col"),
            P("row", "col"),
            P("row", "col"),
            P("row", "col"),
        ),
        out_specs=(P(None, ("row", "col")), P("row", "col"), P("row", "col"), P()),
        check_vma=False,
    )
```

```python
import jax
import jax.numpy as jnp
from jax import lax
from jax.experimental import pallas as pl
from jax.experimental.pallas import tpu as pltpu
from jax.sharding import PartitionSpec as P

N = 64
ROWS = 16
COLS = 8
LOCAL = 128
TILE_ROWS = COLS * LOCAL
TILE_COLS = 2048
OWN = N // ROWS
PIECES = TILE_COLS // 128
HIGHEST = lax.Precision.HIGHEST
F32 = jnp.float32
BF16 = jnp.bfloat16
MIB = 1024 * 1024


def dot(a, b, contract, precision=None):
    return lax.dot_general(
        a, b, ((contract[:1], contract[1:]), ((), ())), precision=precision, preferred_element_type=F32
    )


def split(value):
    high = value.astype(BF16)
    return high, (value - high.astype(F32)).astype(BF16)


def payload_kernel(grad_ref, panel_ref, out_ref):
    grad = grad_ref[...]
    term = dot(grad, panel_ref[...], (1, 1), HIGHEST)
    out_ref[:N, :] = grad
    out_ref[N:, :N] = term[: N // 2]
    out_ref[N:, N:] = term[N // 2 :]


def inverse_kernel(factor_ref, payload_ref, out_ref, copy_ref):
    copy_ref[...] = payload_ref[...]
    factor = factor_ref[...]
    row = lax.broadcasted_iota(jnp.int32, (N, N), 0)
    col = lax.broadcasted_iota(jnp.int32, (N, N), 1)
    eye = jnp.where(row == col, 1.0, 0.0).astype(F32)
    diagonal = jnp.sum(factor * eye, axis=1, keepdims=True)
    diagonal_row = jnp.sum(factor * eye, axis=0, keepdims=True)
    below = jnp.where(row > col, factor, 0.0) / diagonal
    value = eye
    for j in range(N - 1):
        value = value - below[:, j : j + 1] * value[j : j + 1, :]
    out_ref[...] = value / diagonal_row


def product_kernel(
    near_ref, far_ref, inverse_ref, row_panel_ref, trailing_ref,
    own_ref, left_ref, send_ref,
    gathered, rows,
):
    chunk = 256
    place = lax.axis_index("col")
    chip, core = place // 2, lax.rem(place, 2)
    for k in range(4):
        from_chip = lax.rem(chip - k + 4, 4) * 2
        for ref, which in ((near_ref, core), (far_ref, 1 - core)):
            start = pl.multiple_of((from_chip + which) * LOCAL, LOCAL)
            gathered[:, pl.ds(start, LOCAL)] = ref[k, :N, :]
    term = near_ref[0, N:, :] + far_ref[0, N:, :]
    for k in range(1, 4):
        term = term + near_ref[k, N:, :] + far_ref[k, N:, :]
    for j in range(PIECES):
        rows[OWN * j : OWN * (j + 1), :] = row_panel_ref[:, 128 * j : 128 * (j + 1)]
    own_rows = rows[...]
    for s in range(ROWS):
        send_ref[s, N : 2 * N, :] = own_rows
        send_ref[s, 2 * N :, :] = term
    solved = dot(inverse_ref[...], gathered[...], (0, 0), HIGHEST)
    gathered[...] = solved
    own_ref[...] = gathered[:, pl.ds(pl.multiple_of(place * LOCAL, LOCAL), LOCAL)]
    high, low = split(solved)
    both = jnp.concatenate([high, low], axis=0)
    doubled = jnp.concatenate([solved, solved], axis=0).T
    lane = lax.broadcasted_iota(jnp.int32, doubled.shape, 1)
    rounded = doubled.astype(BF16).astype(F32)
    pieces = jnp.where(lane < N, rounded, doubled - rounded).astype(BF16)
    left_ref[:, : 2 * N] = pieces
    left_ref[:, 2 * N :] = pieces
    for i in range(TILE_COLS // chunk):
        t_high, t_low = split(trailing_ref[:, i * chunk : (i + 1) * chunk])
        part = dot(both, t_high, (1, 0)) + dot(both, t_low, (1, 0))
        part = part[:N] + part[N:]
        for s in range(ROWS):
            for jj in range(chunk // 128):
                j = i * (chunk // 128) + jj
                send_ref[s, OWN * j : OWN * (j + 1), :] = part[OWN * s : OWN * (s + 1), 128 * jj : 128 * (jj + 1)]


def update_kernel(
    recv_ref, left_ref, inverse_ref, factor_ref, diag_grad_ref, row_grad_ref, grad_ref,
    out_ref, row_out_ref, diag_out_ref,
    result, full, right, small, out_sems,
):
    count = 8
    height = TILE_ROWS // count
    stores = []
    for i in range(count):
        part = pl.ds(i * height, height)
        stores.append(pltpu.make_async_copy(result.at[part], out_ref.at[part], out_sems.at[i]))
    for s in range(ROWS):
        for j in range(PIECES):
            full[OWN * s : OWN * (s + 1), 128 * j : 128 * (j + 1)] = recv_ref[s, N + OWN * j : N + OWN * (j + 1), :]
    high, low = split(full[...])
    right[:N] = high
    right[N : 2 * N] = high
    right[2 * N : 3 * N] = low
    right[3 * N :] = low

    def step(i):
        part = slice(i * height, (i + 1) * height)
        result[part] = grad_ref[part] - dot(left_ref[part], right[...], (1, 0))
        stores[i].start()

    for i in range(count // 2):
        step(i)

    packed = recv_ref[0, 2 * N :, :]
    reduced = recv_ref[0, :N, :]
    for s in range(1, ROWS):
        packed = packed + recv_ref[s, 2 * N :, :]
        reduced = reduced + recv_ref[s, :N, :]
    total = jnp.concatenate([packed[:, :N], packed[:, N:]], axis=0)
    inverse, factor = inverse_ref[...], factor_ref[...]
    r_id = lax.broadcasted_iota(jnp.int32, (N, N), 0)
    c_id = lax.broadcasted_iota(jnp.int32, (N, N), 1)
    lower = r_id >= c_id
    dsum = diag_grad_ref[...] - jnp.where(lower, dot(inverse, total, (0, 0), HIGHEST), 0.0)
    phi = jnp.where(lower, dot(factor, dsum, (0, 0), HIGHEST), 0.0)
    phi = jnp.where(r_id == c_id, 0.5 * phi, phi)
    spart = dot(dot(inverse, phi, (0, 0), HIGHEST), inverse, (1, 0), HIGHEST)
    both = spart + spart.T
    diag_out_ref[...] = 0.5 * both
    small[...] = both
    own_both = small[pl.ds(lax.axis_index("row") * OWN, OWN), :]
    both_high, both_low = split(own_both)
    wide = jnp.concatenate([both_high, both_low, both_high, both_low], axis=1)
    second = dot(wide, right[...], (1, 0))
    for j in range(PIECES):
        cols = slice(128 * j, 128 * (j + 1))
        row_out_ref[:, cols] = row_grad_ref[:, cols] - reduced[OWN * j : OWN * (j + 1), :] - second[:, cols]

    for i in range(count // 2, count):
        step(i)
    for copy in stores:
        copy.wait()


def across_chips(value, k):
    pairs = [(2 * x + c, 2 * ((x + k) % 4) + c) for x in range(4) for c in range(2)]
    return lax.ppermute(value, "col", pairs)


def per_device(panel_t, panel_grad_t, diag_factor, diag_grad, row_panel, row_grad, trailing, trailing_grad):
    vmem = pl.BlockSpec(memory_space=pltpu.VMEM)
    anywhere = pl.BlockSpec(memory_space=pl.ANY)
    payload = pl.pallas_call(
        payload_kernel,
        out_shape=jax.ShapeDtypeStruct((N + N // 2, LOCAL), F32),
        in_specs=[vmem, vmem],
        out_specs=vmem,
        compiler_params=pltpu.CompilerParams(vmem_limit_bytes=MIB),
        name="payload",
    )(panel_grad_t, panel_t)
    opposite = across_chips(payload, 2)
    right = across_chips(payload, 1)
    left = across_chips(payload, 3)
    inverse, payload = pl.pallas_call(
        inverse_kernel,
        out_shape=(jax.ShapeDtypeStruct((N, N), F32), jax.ShapeDtypeStruct((N + N // 2, LOCAL), F32)),
        in_specs=[vmem, vmem],
        out_specs=(vmem, vmem),
        compiler_params=pltpu.CompilerParams(vmem_limit_bytes=MIB),
        name="inverse",
    )(diag_factor, payload)
    near = jnp.stack([payload, right, opposite, left])
    far = lax.ppermute(near, "col", [(i, i ^ 1) for i in range(COLS)])
    panel_out, left_factor, send = pl.pallas_call(
        product_kernel,
        out_shape=(
            jax.ShapeDtypeStruct((N, LOCAL), F32),
            jax.ShapeDtypeStruct((TILE_ROWS, 4 * N), BF16),
            jax.ShapeDtypeStruct((ROWS, 2 * N + N // 2, 128), F32),
        ),
        in_specs=[vmem] * 5,
        out_specs=(vmem,) * 3,
        scratch_shapes=[
            pltpu.VMEM((N, TILE_ROWS), F32),
            pltpu.VMEM((N, 128), F32),
        ],
        compiler_params=pltpu.CompilerParams(vmem_limit_bytes=24 * MIB),
        name="product",
    )(near, far, inverse, row_panel, trailing)
    recv = lax.all_to_all(send, "row", 0, 0)
    trailing_out, row_out, diag_out = pl.pallas_call(
        update_kernel,
        out_shape=(
            jax.ShapeDtypeStruct((TILE_ROWS, TILE_COLS), F32),
            jax.ShapeDtypeStruct((OWN, TILE_COLS), F32),
            jax.ShapeDtypeStruct((N, N), F32),
        ),
        in_specs=[vmem] * 7,
        out_specs=(anywhere, vmem, vmem),
        scratch_shapes=[
            pltpu.VMEM((TILE_ROWS, TILE_COLS), F32),
            pltpu.VMEM((N, TILE_COLS), F32),
            pltpu.VMEM((4 * N, TILE_COLS), BF16),
            pltpu.VMEM((N, N), F32),
            pltpu.SemaphoreType.DMA((8,)),
        ],
        compiler_params=pltpu.CompilerParams(vmem_limit_bytes=32 * MIB),
        name="update",
    )(recv, left_factor, inverse, diag_factor, diag_grad, row_grad, trailing_grad)
    return (panel_out, trailing_out, row_out, diag_out)


def solution(mesh):
    return jax.shard_map(
        per_device,
        mesh=mesh,
        in_specs=(
            P(None, ("row", "col")),
            P(None, ("row", "col")),
            P(),
            P(),
            P("row", "col"),
            P("row", "col"),
            P("row", "col"),
            P("row", "col"),
        ),
        out_specs=(P(None, ("row", "col")), P("row", "col"), P("row", "col"), P()),
        check_vma=False,
    )
```

```python
import jax
import jax.numpy as jnp
from jax import lax
from jax.experimental import pallas as pl
from jax.experimental.pallas import tpu as pltpu
from jax.sharding import PartitionSpec as P

N = 64
ROWS = 16
COLS = 8
LOCAL = 128
TILE_ROWS = COLS * LOCAL
TILE_COLS = 2048
OWN = N // ROWS
PIECES = TILE_COLS // 128
HIGHEST = lax.Precision.HIGHEST
F32 = jnp.float32
BF16 = jnp.bfloat16
MIB = 1024 * 1024


def dot(a, b, contract, precision=None):
    return lax.dot_general(
        a, b, ((contract[:1], contract[1:]), ((), ())), precision=precision, preferred_element_type=F32
    )


def split(value):
    high = value.astype(BF16)
    return high, (value - high.astype(F32)).astype(BF16)


def block_row(k, other):
    place = lax.axis_index("col")
    chip, core = place // 2, lax.rem(place, 2)
    core = 1 - core if other else core
    return pl.multiple_of((lax.rem(chip - k + 4, 4) * 2 + core) * LOCAL, LOCAL)


def prepare_kernel(
    payload_ref, factor_ref, row_panel_ref,
    inverse_ref, copy_ref, rows_ref,
):
    copy_ref[...] = payload_ref[...]
    factor = factor_ref[...]
    row = lax.broadcasted_iota(jnp.int32, (N, N), 0)
    col = lax.broadcasted_iota(jnp.int32, (N, N), 1)
    eye = jnp.where(row == col, 1.0, 0.0).astype(F32)
    diagonal = jnp.sum(factor * eye, axis=1, keepdims=True)
    diagonal_row = jnp.sum(factor * eye, axis=0, keepdims=True)
    below = jnp.where(row > col, factor, 0.0) / diagonal
    value = eye
    for j in range(N - 1):
        value = value - below[:, j : j + 1] * value[j : j + 1, :]
    inverse_ref[...] = value / diagonal_row
    for j in range(PIECES):
        rows_ref[OWN * j : OWN * (j + 1), :] = row_panel_ref[:, 128 * j : 128 * (j + 1)]


def solve_line(line_ref, inverse_ref, left_ref):
    grads = jnp.concatenate([line_ref[k, :N, :] for k in range(4)], axis=1)
    panels = jnp.concatenate([line_ref[k, N:, :] for k in range(4)], axis=1)
    solved = dot(inverse_ref[...], grads, (0, 0), HIGHEST)
    high, low = split(solved)
    both = jnp.concatenate([high, low], axis=0)
    panel_high, panel_low = split(panels)
    term = dot(both, panel_high, (1, 1)) + dot(both, panel_low, (1, 1))
    doubled = jnp.concatenate([solved, solved], axis=0).T
    lane = lax.broadcasted_iota(jnp.int32, doubled.shape, 1)
    rounded = doubled.astype(BF16).astype(F32)
    pieces = jnp.where(lane < N, rounded, doubled - rounded).astype(BF16)
    left_ref[:, : 2 * N] = pieces
    left_ref[:, 2 * N :] = pieces
    return solved, both, term[:N] + term[N:]


def line_product(both, tile_ref, cols, other):
    tile = jnp.concatenate([tile_ref[pl.ds(block_row(k, other), LOCAL), cols] for k in range(4)], axis=0)
    t_high, t_low = split(tile)
    part = dot(both, t_high, (1, 0)) + dot(both, t_low, (1, 0))
    return part[:N] + part[N:]


CHUNK = 256


def near_kernel(
    near_ref, inverse_ref, tile_ref,
    own_ref, left_ref, term_ref, part_ref,
):
    solved, both, term = solve_line(near_ref, inverse_ref, left_ref)
    own_ref[...] = solved[:, :LOCAL]
    term_ref[...] = term
    for i in range(TILE_COLS // CHUNK):
        cols = slice(i * CHUNK, (i + 1) * CHUNK)
        part_ref[:, cols] = line_product(both, tile_ref, cols, False)


def far_kernel(
    far_ref, inverse_ref, rows_ref, tile_ref, near_term_ref, near_part_ref,
    left_ref, send_ref,
):
    own_rows = rows_ref[...]
    for s in range(ROWS):
        send_ref[s, N : 2 * N, :] = own_rows
    _, both, term = solve_line(far_ref, inverse_ref, left_ref)
    term = term + near_term_ref[...]
    packed = jnp.concatenate([term[: N // 2], term[N // 2 :]], axis=1)
    for s in range(ROWS):
        send_ref[s, 2 * N :, :] = packed
    for i in range(TILE_COLS // CHUNK):
        cols = slice(i * CHUNK, (i + 1) * CHUNK)
        part = near_part_ref[:, cols] + line_product(both, tile_ref, cols, True)
        for s in range(ROWS):
            for jj in range(CHUNK // 128):
                j = i * (CHUNK // 128) + jj
                send_ref[s, OWN * j : OWN * (j + 1), :] = part[OWN * s : OWN * (s + 1), 128 * jj : 128 * (jj + 1)]


def update_kernel(
    recv_ref, near_left_ref, far_left_ref, inverse_ref, factor_ref, diag_grad_ref, row_grad_ref, grad_ref,
    out_ref, row_out_ref, diag_out_ref,
    result, full, right, small, out_sems,
):
    for s in range(ROWS):
        for j in range(PIECES):
            full[OWN * s : OWN * (s + 1), 128 * j : 128 * (j + 1)] = recv_ref[s, N + OWN * j : N + OWN * (j + 1), :]
    high, low = split(full[...])
    right[:N] = high
    right[N : 2 * N] = high
    right[2 * N : 3 * N] = low
    right[3 * N :] = low
    stores = []

    def step(left_ref, k, other):
        part = pl.ds(block_row(k, other), LOCAL)
        result[part] = grad_ref[part] - dot(left_ref[k * LOCAL : (k + 1) * LOCAL], right[...], (1, 0))
        stores.append(pltpu.make_async_copy(result.at[part], out_ref.at[part], out_sems.at[len(stores)]))
        stores[-1].start()

    for k in range(4):
        step(near_left_ref, k, False)

    packed = recv_ref[0, 2 * N :, :]
    reduced = recv_ref[0, :N, :]
    for s in range(1, ROWS):
        packed = packed + recv_ref[s, 2 * N :, :]
        reduced = reduced + recv_ref[s, :N, :]
    total = jnp.concatenate([packed[:, :N], packed[:, N:]], axis=0)
    inverse, factor = inverse_ref[...], factor_ref[...]
    r_id = lax.broadcasted_iota(jnp.int32, (N, N), 0)
    c_id = lax.broadcasted_iota(jnp.int32, (N, N), 1)
    lower = r_id >= c_id
    dsum = diag_grad_ref[...] - jnp.where(lower, total, 0.0)
    phi = jnp.where(lower, dot(factor, dsum, (0, 0), HIGHEST), 0.0)
    phi = jnp.where(r_id == c_id, 0.5 * phi, phi)
    spart = dot(dot(inverse, phi, (0, 0), HIGHEST), inverse, (1, 0), HIGHEST)
    both = spart + spart.T
    diag_out_ref[...] = 0.5 * both
    small[...] = both
    own_both = small[pl.ds(lax.axis_index("row") * OWN, OWN), :]
    both_high, both_low = split(own_both)
    wide = jnp.concatenate([both_high, both_low, both_high, both_low], axis=1)
    second = dot(wide, right[...], (1, 0))
    for j in range(PIECES):
        cols = slice(128 * j, 128 * (j + 1))
        row_out_ref[:, cols] = row_grad_ref[:, cols] - reduced[OWN * j : OWN * (j + 1), :] - second[:, cols]

    for k in range(4):
        step(far_left_ref, k, True)
    for copy in stores:
        copy.wait()


def across_chips(value, k):
    pairs = [(2 * x + c, 2 * ((x + k) % 4) + c) for x in range(4) for c in range(2)]
    return lax.ppermute(value, "col", pairs)


def per_device(panel_t, panel_grad_t, diag_factor, diag_grad, row_panel, row_grad, trailing, trailing_grad):
    vmem = pl.BlockSpec(memory_space=pltpu.VMEM)
    anywhere = pl.BlockSpec(memory_space=pl.ANY)
    payload = jnp.pad(panel_grad_t, ((0, N), (0, 0))) + jnp.pad(panel_t, ((N, 0), (0, 0)))
    opposite = across_chips(payload, 2)
    right = across_chips(payload, 1)
    left = across_chips(payload, 3)
    inverse, payload, rows = pl.pallas_call(
        prepare_kernel,
        out_shape=(
            jax.ShapeDtypeStruct((N, N), F32),
            jax.ShapeDtypeStruct((2 * N, LOCAL), F32),
            jax.ShapeDtypeStruct((N, 128), F32),
        ),
        in_specs=[vmem] * 3,
        out_specs=(vmem,) * 3,
        compiler_params=pltpu.CompilerParams(vmem_limit_bytes=4 * MIB),
        cost_estimate=pl.CostEstimate(flops=4_000_000_000, bytes_accessed=0, transcendentals=0),
        name="prepare",
    )(payload, diag_factor, row_panel)
    near = jnp.stack([payload, right, opposite, left])
    far = lax.ppermute(near, "col", [(i, i ^ 1) for i in range(COLS)])
    panel_out, near_left, near_term, near_part = pl.pallas_call(
        near_kernel,
        out_shape=(
            jax.ShapeDtypeStruct((N, LOCAL), F32),
            jax.ShapeDtypeStruct((TILE_ROWS // 2, 4 * N), BF16),
            jax.ShapeDtypeStruct((N, N), F32),
            jax.ShapeDtypeStruct((N, TILE_COLS), F32),
        ),
        in_specs=[vmem] * 3,
        out_specs=(vmem,) * 4,
        compiler_params=pltpu.CompilerParams(vmem_limit_bytes=16 * MIB),
        cost_estimate=pl.CostEstimate(flops=1_000_000_000, bytes_accessed=0, transcendentals=0),
        name="near",
    )(near, inverse, trailing)
    far_left, send = pl.pallas_call(
        far_kernel,
        out_shape=(
            jax.ShapeDtypeStruct((TILE_ROWS // 2, 4 * N), BF16),
            jax.ShapeDtypeStruct((ROWS, 2 * N + N // 2, 128), F32),
        ),
        in_specs=[vmem] * 6,
        out_specs=(vmem,) * 2,
        compiler_params=pltpu.CompilerParams(vmem_limit_bytes=16 * MIB),
        name="far",
    )(far, inverse, rows, trailing, near_term, near_part)
    recv = lax.all_to_all(send, "row", 0, 0)
    trailing_out, row_out, diag_out = pl.pallas_call(
        update_kernel,
        out_shape=(
            jax.ShapeDtypeStruct((TILE_ROWS, TILE_COLS), F32),
            jax.ShapeDtypeStruct((OWN, TILE_COLS), F32),
            jax.ShapeDtypeStruct((N, N), F32),
        ),
        in_specs=[vmem] * 8,
        out_specs=(anywhere, vmem, vmem),
        scratch_shapes=[
            pltpu.VMEM((TILE_ROWS, TILE_COLS), F32),
            pltpu.VMEM((N, TILE_COLS), F32),
            pltpu.VMEM((4 * N, TILE_COLS), BF16),
            pltpu.VMEM((N, N), F32),
            pltpu.SemaphoreType.DMA((8,)),
        ],
        compiler_params=pltpu.CompilerParams(vmem_limit_bytes=32 * MIB),
        name="update",
    )(recv, near_left, far_left, inverse, diag_factor, diag_grad, row_grad, trailing_grad)
    return (panel_out, trailing_out, row_out, diag_out)


def solution(mesh):
    return jax.shard_map(
        per_device,
        mesh=mesh,
        in_specs=(
            P(None, ("row", "col")),
            P(None, ("row", "col")),
            P(),
            P(),
            P("row", "col"),
            P("row", "col"),
            P("row", "col"),
            P("row", "col"),
        ),
        out_specs=(P(None, ("row", "col")), P("row", "col"), P("row", "col"), P()),
        check_vma=False,
    )
```

```python
import jax
import jax.numpy as jnp
from jax import lax
from jax.experimental import pallas as pl
from jax.experimental.pallas import tpu as pltpu
from jax.sharding import PartitionSpec as P

N = 64
ROWS = 16
COLS = 8
LOCAL = 128
TILE_ROWS = COLS * LOCAL
TILE_COLS = 2048
OWN = N // ROWS
PIECES = TILE_COLS // 128
HIGHEST = lax.Precision.HIGHEST
F32 = jnp.float32
BF16 = jnp.bfloat16
MIB = 1024 * 1024


def dot(a, b, contract, precision=None):
    return lax.dot_general(
        a, b, ((contract[:1], contract[1:]), ((), ())), precision=precision, preferred_element_type=F32
    )


def split(value):
    high = value.astype(BF16)
    return high, (value - high.astype(F32)).astype(BF16)


def block_row(k, other):
    place = lax.axis_index("col")
    chip, core = place // 2, lax.rem(place, 2)
    core = 1 - core if other else core
    return pl.multiple_of((lax.rem(chip - k + 4, 4) * 2 + core) * LOCAL, LOCAL)


def prepare_kernel(
    payload_ref, factor_ref, row_panel_ref,
    inverse_ref, copy_ref, rows_ref,
):
    copy_ref[...] = payload_ref[...]
    factor = factor_ref[...]
    row = lax.broadcasted_iota(jnp.int32, (N, N), 0)
    col = lax.broadcasted_iota(jnp.int32, (N, N), 1)
    eye = jnp.where(row == col, 1.0, 0.0).astype(F32)
    diagonal = jnp.sum(factor * eye, axis=1, keepdims=True)
    diagonal_row = jnp.sum(factor * eye, axis=0, keepdims=True)
    below = jnp.where(row > col, factor, 0.0) / diagonal
    value = eye
    for j in range(N - 1):
        value = value - below[:, j : j + 1] * value[j : j + 1, :]
    inverse_ref[...] = value / diagonal_row
    for j in range(PIECES):
        rows_ref[OWN * j : OWN * (j + 1), :] = row_panel_ref[:, 128 * j : 128 * (j + 1)]


def solve_line(line_ref, inverse_ref, left_ref, first):
    grads = jnp.concatenate([line_ref[k, :N, :] for k in range(4)], axis=1)
    panels = jnp.concatenate([line_ref[k, N:, :] for k in range(4)], axis=1)
    solved = dot(inverse_ref[...], grads, (0, 0), HIGHEST)
    high, low = split(solved)
    both = jnp.concatenate([high, low], axis=0)
    panel_high, panel_low = split(panels)
    term = dot(both, panel_high, (1, 1)) + dot(both, panel_low, (1, 1))
    doubled = jnp.concatenate([solved, solved], axis=0).T
    lane = lax.broadcasted_iota(jnp.int32, doubled.shape, 1)
    rounded = doubled.astype(BF16).astype(F32)
    pieces = jnp.where(lane < N, rounded, doubled - rounded).astype(BF16)
    part = slice(first, first + TILE_ROWS // 2)
    left_ref[part, : 2 * N] = pieces
    left_ref[part, 2 * N :] = pieces
    return solved, both, term[:N] + term[N:]


def line_product(both, tile_ref, cols, other):
    tile = jnp.concatenate([tile_ref[pl.ds(block_row(k, other), LOCAL), cols] for k in range(4)], axis=0)
    t_high, t_low = split(tile)
    part = dot(both, t_high, (1, 0)) + dot(both, t_low, (1, 0))
    return part[:N] + part[N:]


CHUNK = 256
HALF = N // 2
PACKED = 3 * HALF * HALF // 128


def pack_lower(term):
    blocks = jnp.concatenate([term[:HALF, :HALF], term[HALF:, :HALF], term[HALF:, HALF:]], axis=1)
    rest = jnp.concatenate([blocks[PACKED:, HALF * i : HALF * (i + 1)] for i in range(3)], axis=0)
    return jnp.concatenate([blocks[:PACKED], rest], axis=1)


def unpack_lower(packed):
    step = HALF - PACKED
    rest = jnp.concatenate([packed[step * i : step * (i + 1), 3 * HALF :] for i in range(3)], axis=1)
    blocks = jnp.concatenate([packed[:, : 3 * HALF], rest], axis=0)
    top = jnp.concatenate([blocks[:, :HALF], jnp.zeros((HALF, HALF), F32)], axis=1)
    return jnp.concatenate([top, blocks[:, HALF:]], axis=0)


def near_kernel(
    near_ref, inverse_ref, tile_ref,
    own_hbm, left_ref, term_ref, part_ref,
    own, sem,
):
    solved, both, term = solve_line(near_ref, inverse_ref, left_ref, 0)
    own[...] = solved[:, :LOCAL]
    copy = pltpu.make_async_copy(own, own_hbm, sem)
    copy.start()
    term_ref[...] = term
    for i in range(TILE_COLS // CHUNK):
        cols = slice(i * CHUNK, (i + 1) * CHUNK)
        part_ref[:, cols] = line_product(both, tile_ref, cols, False)
    copy.wait()


def far_kernel(
    far_ref, inverse_ref, rows_ref, tile_ref, near_term_ref, near_part_ref, near_left_ref,
    left_ref, send_ref,
):
    own_rows = rows_ref[...]
    for s in range(ROWS):
        send_ref[s, N : 2 * N, :] = own_rows
    _, both, term = solve_line(far_ref, inverse_ref, left_ref, TILE_ROWS // 2)
    term = term + near_term_ref[...]
    packed = pack_lower(term)
    for s in range(ROWS):
        send_ref[s, 2 * N :, :] = packed
    for i in range(TILE_COLS // CHUNK):
        cols = slice(i * CHUNK, (i + 1) * CHUNK)
        part = near_part_ref[:, cols] + line_product(both, tile_ref, cols, True)
        for s in range(ROWS):
            for jj in range(CHUNK // 128):
                j = i * (CHUNK // 128) + jj
                send_ref[s, OWN * j : OWN * (j + 1), :] = part[OWN * s : OWN * (s + 1), 128 * jj : 128 * (jj + 1)]


def update_kernel(
    recv_ref, left, inverse_ref, factor_ref, diag_grad_ref, row_grad_ref, grad_ref,
    out_ref, row_out_hbm, diag_out_hbm,
    result, full, right, small, row_out, diag_out, out_sems, small_sems,
):
    stores = []
    edges = [0, 256, 512, 768, 1024, 1280, 1536, 1792, 2048]

    def step(i):
        cols = slice(edges[i], edges[i + 1])
        for s in range(ROWS):
            for j in range(edges[i] // 128, edges[i + 1] // 128):
                full[OWN * s : OWN * (s + 1), 128 * j : 128 * (j + 1)] = recv_ref[s, N + OWN * j : N + OWN * (j + 1), :]
        high, low = split(full[:, cols])
        right[:, cols] = jnp.concatenate([high, high, low, low], axis=0)
        product = dot(left[...], right[:, cols], (1, 0))
        for slot in range(COLS):
            part = pl.ds(block_row(slot % 4, slot >= 4), LOCAL)
            result[part, cols] = grad_ref[part, cols] - product[slot * LOCAL : (slot + 1) * LOCAL]
        stores.append(pltpu.make_async_copy(result.at[:, cols], out_ref.at[:, cols], out_sems.at[i]))
        stores[-1].start()

    count = len(edges) - 1
    for i in range(4):
        step(i)

    packed = recv_ref[0, 2 * N :, :]
    reduced = recv_ref[0, :N, :]
    for s in range(1, ROWS):
        packed = packed + recv_ref[s, 2 * N :, :]
        reduced = reduced + recv_ref[s, :N, :]
    total = unpack_lower(packed)
    inverse, factor = inverse_ref[...], factor_ref[...]
    r_id = lax.broadcasted_iota(jnp.int32, (N, N), 0)
    c_id = lax.broadcasted_iota(jnp.int32, (N, N), 1)
    lower = r_id >= c_id
    dsum = diag_grad_ref[...] - jnp.where(lower, total, 0.0)
    phi = jnp.where(lower, dot(factor, dsum, (0, 0), HIGHEST), 0.0)
    phi = jnp.where(r_id == c_id, 0.5 * phi, phi)
    spart = dot(dot(inverse, phi, (0, 0), HIGHEST), inverse, (1, 0), HIGHEST)
    both = spart + spart.T
    diag_out[...] = 0.5 * both
    stores.append(pltpu.make_async_copy(diag_out, diag_out_hbm, small_sems.at[0]))
    stores[-1].start()
    small[...] = both
    own_both = small[pl.ds(lax.axis_index("row") * OWN, OWN), :]
    both_high, both_low = split(own_both)
    wide = jnp.concatenate([both_high, both_low, both_high, both_low], axis=1)

    for i in range(4, count):
        step(i)
    second = dot(wide, right[...], (1, 0))
    for j in range(PIECES):
        cols = slice(128 * j, 128 * (j + 1))
        row_out[:, cols] = row_grad_ref[:, cols] - reduced[OWN * j : OWN * (j + 1), :] - second[:, cols]
    stores.append(pltpu.make_async_copy(row_out, row_out_hbm, small_sems.at[1]))
    stores[-1].start()
    for copy in stores:
        copy.wait()


def across_chips(value, k):
    pairs = [(2 * x + c, 2 * ((x + k) % 4) + c) for x in range(4) for c in range(2)]
    return lax.ppermute(value, "col", pairs)


def per_device(panel_t, panel_grad_t, diag_factor, diag_grad, row_panel, row_grad, trailing, trailing_grad):
    vmem = pl.BlockSpec(memory_space=pltpu.VMEM)
    anywhere = pl.BlockSpec(memory_space=pl.ANY)
    payload = jnp.pad(panel_grad_t, ((0, N), (0, 0))) + jnp.pad(panel_t, ((N, 0), (0, 0)))
    opposite = across_chips(payload, 2)
    right = across_chips(payload, 1)
    left = across_chips(payload, 3)
    inverse, payload, rows = pl.pallas_call(
        prepare_kernel,
        out_shape=(
            jax.ShapeDtypeStruct((N, N), F32),
            jax.ShapeDtypeStruct((2 * N, LOCAL), F32),
            jax.ShapeDtypeStruct((N, 128), F32),
        ),
        in_specs=[vmem] * 3,
        out_specs=(vmem,) * 3,
        compiler_params=pltpu.CompilerParams(vmem_limit_bytes=4 * MIB),
        cost_estimate=pl.CostEstimate(flops=4_000_000_000, bytes_accessed=0, transcendentals=0),
        name="prepare",
    )(payload, diag_factor, row_panel)
    near = jnp.stack([payload, right, opposite, left])
    far = lax.ppermute(near, "col", [(i, i ^ 1) for i in range(COLS)])
    panel_out, left_factor, near_term, near_part = pl.pallas_call(
        near_kernel,
        out_shape=(
            jax.ShapeDtypeStruct((N, LOCAL), F32),
            jax.ShapeDtypeStruct((TILE_ROWS, 4 * N), BF16),
            jax.ShapeDtypeStruct((N, N), F32),
            jax.ShapeDtypeStruct((N, TILE_COLS), F32),
        ),
        in_specs=[vmem] * 3,
        out_specs=(anywhere,) + (vmem,) * 3,
        scratch_shapes=[pltpu.VMEM((N, LOCAL), F32), pltpu.SemaphoreType.DMA],
        compiler_params=pltpu.CompilerParams(vmem_limit_bytes=16 * MIB),
        cost_estimate=pl.CostEstimate(flops=1_000_000_000, bytes_accessed=0, transcendentals=0),
        name="near",
    )(near, inverse, trailing)
    left_factor, send = pl.pallas_call(
        far_kernel,
        out_shape=(
            jax.ShapeDtypeStruct((TILE_ROWS, 4 * N), BF16),
            jax.ShapeDtypeStruct((ROWS, 2 * N + PACKED, 128), F32),
        ),
        in_specs=[vmem] * 6 + [anywhere],
        out_specs=(vmem,) * 2,
        input_output_aliases={6: 0},
        compiler_params=pltpu.CompilerParams(vmem_limit_bytes=16 * MIB),
        name="far",
    )(far, inverse, rows, trailing, near_term, near_part, left_factor)
    recv = lax.all_to_all(send, "row", 0, 0)
    trailing_out, row_out, diag_out = pl.pallas_call(
        update_kernel,
        out_shape=(
            jax.ShapeDtypeStruct((TILE_ROWS, TILE_COLS), F32),
            jax.ShapeDtypeStruct((OWN, TILE_COLS), F32),
            jax.ShapeDtypeStruct((N, N), F32),
        ),
        in_specs=[vmem] * 7,
        out_specs=(anywhere,) * 3,
        scratch_shapes=[
            pltpu.VMEM((TILE_ROWS, TILE_COLS), F32),
            pltpu.VMEM((N, TILE_COLS), F32),
            pltpu.VMEM((4 * N, TILE_COLS), BF16),
            pltpu.VMEM((N, N), F32),
            pltpu.VMEM((OWN, TILE_COLS), F32),
            pltpu.VMEM((N, N), F32),
            pltpu.SemaphoreType.DMA((8,)),
            pltpu.SemaphoreType.DMA((2,)),
        ],
        compiler_params=pltpu.CompilerParams(vmem_limit_bytes=32 * MIB),
        name="update",
    )(recv, left_factor, inverse, diag_factor, diag_grad, row_grad, trailing_grad)
    return (panel_out, trailing_out, row_out, diag_out)


def solution(mesh):
    return jax.shard_map(
        per_device,
        mesh=mesh,
        in_specs=(
            P(None, ("row", "col")),
            P(None, ("row", "col")),
            P(),
            P(),
            P("row", "col"),
            P("row", "col"),
            P("row", "col"),
            P("row", "col"),
        ),
        out_specs=(P(None, ("row", "col")), P("row", "col"), P("row", "col"), P()),
        check_vma=False,
    )
```

```python
import jax
import jax.numpy as jnp
from jax import lax
from jax.experimental import pallas as pl
from jax.experimental.pallas import tpu as pltpu
from jax.sharding import PartitionSpec as P

N = 64
ROWS = 16
COLS = 8
LOCAL = 128
TILE_ROWS = COLS * LOCAL
TILE_COLS = 2048
OWN = N // ROWS
PIECES = TILE_COLS // 128
ORDER = [15, 14, 13, 12, 11, 10, 9, 8, 7, 6, 5, 4, 3, 2, 1, 0]
SLOT = [15, 14, 13, 12, 11, 10, 9, 8, 7, 6, 5, 4, 3, 2, 1, 0]
HIGHEST = lax.Precision.HIGHEST
F32 = jnp.float32
BF16 = jnp.bfloat16
MIB = 1024 * 1024


def dot(a, b, contract, precision=None):
    return lax.dot_general(
        a, b, ((contract[:1], contract[1:]), ((), ())), precision=precision, preferred_element_type=F32
    )


def split(value):
    high = value.astype(BF16)
    return high, (value - high.astype(F32)).astype(BF16)


def block_row(k, other):
    place = lax.axis_index("col")
    chip, core = place // 2, lax.rem(place, 2)
    core = 1 - core if other else core
    return pl.multiple_of((lax.rem(chip - k + 4, 4) * 2 + core) * LOCAL, LOCAL)


def prepare_kernel(
    payload_ref, factor_ref, row_panel_ref,
    inverse_ref, copy_ref, rows_ref,
):
    copy_ref[...] = payload_ref[...]
    factor = factor_ref[...]
    row = lax.broadcasted_iota(jnp.int32, (N, N), 0)
    col = lax.broadcasted_iota(jnp.int32, (N, N), 1)
    eye = jnp.where(row == col, 1.0, 0.0).astype(F32)
    diagonal = jnp.sum(factor * eye, axis=1, keepdims=True)
    diagonal_row = jnp.sum(factor * eye, axis=0, keepdims=True)
    below = jnp.where(row > col, factor, 0.0) / diagonal
    value = eye
    for j in range(N - 1):
        value = value - below[:, j : j + 1] * value[j : j + 1, :]
    inverse_ref[...] = value / diagonal_row
    for j in range(PIECES):
        rows_ref[OWN * j : OWN * (j + 1), :] = row_panel_ref[:, 128 * j : 128 * (j + 1)]


def solve_line(line_ref, inverse_ref, left_ref, first):
    grads = jnp.concatenate([line_ref[k, :N, :] for k in range(4)], axis=1)
    panels = jnp.concatenate([line_ref[k, N:, :] for k in range(4)], axis=1)
    solved = dot(inverse_ref[...], grads, (0, 0), HIGHEST)
    high, low = split(solved)
    both = jnp.concatenate([high, low], axis=0)
    panel_high, panel_low = split(panels)
    term = dot(both, panel_high, (1, 1)) + dot(both, panel_low, (1, 1))
    doubled = jnp.concatenate([solved, solved], axis=0).T
    lane = lax.broadcasted_iota(jnp.int32, doubled.shape, 1)
    rounded = doubled.astype(BF16).astype(F32)
    pieces = jnp.where(lane < N, rounded, doubled - rounded).astype(BF16)
    part = slice(first, first + TILE_ROWS // 2)
    left_ref[part, : 2 * N] = pieces
    left_ref[part, 2 * N :] = pieces
    return solved, both, term[:N] + term[N:]


def line_product(both, tile_ref, cols, other):
    tile = jnp.concatenate([tile_ref[pl.ds(block_row(k, other), LOCAL), cols] for k in range(4)], axis=0)
    t_high, t_low = split(tile)
    part = dot(both, t_high, (1, 0)) + dot(both, t_low, (1, 0))
    return part[:N] + part[N:]


CHUNK = 256
HALF = N // 2
PACKED = 3 * HALF * HALF // 128


def pack_lower(term):
    blocks = jnp.concatenate([term[:HALF, :HALF], term[HALF:, :HALF], term[HALF:, HALF:]], axis=1)
    rest = jnp.concatenate([blocks[PACKED:, HALF * i : HALF * (i + 1)] for i in range(3)], axis=0)
    return jnp.concatenate([blocks[:PACKED], rest], axis=1)


def unpack_lower(packed):
    step = HALF - PACKED
    rest = jnp.concatenate([packed[step * i : step * (i + 1), 3 * HALF :] for i in range(3)], axis=1)
    blocks = jnp.concatenate([packed[:, : 3 * HALF], rest], axis=0)
    top = jnp.concatenate([blocks[:, :HALF], jnp.zeros((HALF, HALF), F32)], axis=1)
    return jnp.concatenate([top, blocks[:, HALF:]], axis=0)


def near_kernel(
    near_ref, inverse_ref, tile_ref,
    own_hbm, left_ref, term_ref, part_ref,
    own, sem,
):
    solved, both, term = solve_line(near_ref, inverse_ref, left_ref, 0)
    own[...] = solved[:, :LOCAL]
    copy = pltpu.make_async_copy(own, own_hbm, sem)
    copy.start()
    term_ref[...] = term
    for i in range(TILE_COLS // CHUNK):
        cols = slice(i * CHUNK, (i + 1) * CHUNK)
        part_ref[:, cols] = line_product(both, tile_ref, cols, False)
    copy.wait()


def far_kernel(
    far_ref, inverse_ref, rows_ref, tile_ref, near_term_ref, near_part_ref, near_left_ref,
    left_ref, send_ref,
):
    own_rows = rows_ref[...]
    for s in range(ROWS):
        send_ref[s, N : 2 * N, :] = own_rows
    _, both, term = solve_line(far_ref, inverse_ref, left_ref, TILE_ROWS // 2)
    term = term + near_term_ref[...]
    packed = pack_lower(term)
    for s in range(ROWS):
        send_ref[s, 2 * N :, :] = packed
    for i in range(TILE_COLS // CHUNK):
        cols = slice(i * CHUNK, (i + 1) * CHUNK)
        part = near_part_ref[:, cols] + line_product(both, tile_ref, cols, True)
        for s in range(ROWS):
            for jj in range(CHUNK // 128):
                j = i * (CHUNK // 128) + jj
                send_ref[SLOT[s], OWN * j : OWN * (j + 1), :] = part[OWN * s : OWN * (s + 1), 128 * jj : 128 * (jj + 1)]


def update_kernel(
    recv_ref, left, inverse_ref, factor_ref, diag_grad_ref, row_grad_ref, grad_ref,
    out_ref, row_out_hbm, diag_out_hbm,
    result, full, right, small, row_out, diag_out, out_sems, small_sems,
):
    stores = []
    edges = [0, 256, 512, 768, 1024, 1280, 1536, 1792, 2048]

    def step(i):
        cols = slice(edges[i], edges[i + 1])
        for s in range(ROWS):
            for j in range(edges[i] // 128, edges[i + 1] // 128):
                full[OWN * s : OWN * (s + 1), 128 * j : 128 * (j + 1)] = recv_ref[SLOT[s], N + OWN * j : N + OWN * (j + 1), :]
        high, low = split(full[:, cols])
        right[:, cols] = jnp.concatenate([high, high, low, low], axis=0)
        product = dot(left[...], right[:, cols], (1, 0))
        for slot in range(COLS):
            part = pl.ds(block_row(slot % 4, slot >= 4), LOCAL)
            result[part, cols] = grad_ref[part, cols] - product[slot * LOCAL : (slot + 1) * LOCAL]
        stores.append(pltpu.make_async_copy(result.at[:, cols], out_ref.at[:, cols], out_sems.at[i]))
        stores[-1].start()

    count = len(edges) - 1
    for i in range(4):
        step(i)

    packed = recv_ref[0, 2 * N :, :]
    reduced = recv_ref[0, :N, :]
    for s in range(1, ROWS):
        packed = packed + recv_ref[s, 2 * N :, :]
        reduced = reduced + recv_ref[s, :N, :]
    total = unpack_lower(packed)
    inverse, factor = inverse_ref[...], factor_ref[...]
    r_id = lax.broadcasted_iota(jnp.int32, (N, N), 0)
    c_id = lax.broadcasted_iota(jnp.int32, (N, N), 1)
    lower = r_id >= c_id
    dsum = diag_grad_ref[...] - jnp.where(lower, total, 0.0)
    phi = jnp.where(lower, dot(factor, dsum, (0, 0), HIGHEST), 0.0)
    phi = jnp.where(r_id == c_id, 0.5 * phi, phi)
    spart = dot(dot(inverse, phi, (0, 0), HIGHEST), inverse, (1, 0), HIGHEST)
    both = spart + spart.T
    diag_out[...] = 0.5 * both
    stores.append(pltpu.make_async_copy(diag_out, diag_out_hbm, small_sems.at[0]))
    stores[-1].start()
    small[...] = both
    own_both = small[pl.ds(lax.axis_index("row") * OWN, OWN), :]
    both_high, both_low = split(own_both)
    wide = jnp.concatenate([both_high, both_low, both_high, both_low], axis=1)

    for i in range(4, count):
        step(i)
    second = dot(wide, right[...], (1, 0))
    for j in range(PIECES):
        cols = slice(128 * j, 128 * (j + 1))
        row_out[:, cols] = row_grad_ref[:, cols] - reduced[OWN * j : OWN * (j + 1), :] - second[:, cols]
    stores.append(pltpu.make_async_copy(row_out, row_out_hbm, small_sems.at[1]))
    stores[-1].start()
    for copy in stores:
        copy.wait()


def across_chips(value, k):
    pairs = [(2 * x + c, 2 * ((x + k) % 4) + c) for x in range(4) for c in range(2)]
    return lax.ppermute(value, "col", pairs)


def per_device(panel_t, panel_grad_t, diag_factor, diag_grad, row_panel, row_grad, trailing, trailing_grad):
    vmem = pl.BlockSpec(memory_space=pltpu.VMEM)
    anywhere = pl.BlockSpec(memory_space=pl.ANY)
    payload = jnp.pad(panel_grad_t, ((0, N), (0, 0))) + jnp.pad(panel_t, ((N, 0), (0, 0)))
    opposite = across_chips(payload, 2)
    right = across_chips(payload, 1)
    left = across_chips(payload, 3)
    inverse, payload, rows = pl.pallas_call(
        prepare_kernel,
        out_shape=(
            jax.ShapeDtypeStruct((N, N), F32),
            jax.ShapeDtypeStruct((2 * N, LOCAL), F32),
            jax.ShapeDtypeStruct((N, 128), F32),
        ),
        in_specs=[vmem] * 3,
        out_specs=(vmem,) * 3,
        compiler_params=pltpu.CompilerParams(vmem_limit_bytes=4 * MIB),
        cost_estimate=pl.CostEstimate(flops=4_000_000_000, bytes_accessed=0, transcendentals=0),
        name="prepare",
    )(payload, diag_factor, row_panel)
    near = jnp.stack([payload, right, opposite, left])
    far = lax.ppermute(near, "col", [(i, i ^ 1) for i in range(COLS)])
    panel_out, left_factor, near_term, near_part = pl.pallas_call(
        near_kernel,
        out_shape=(
            jax.ShapeDtypeStruct((N, LOCAL), F32),
            jax.ShapeDtypeStruct((TILE_ROWS, 4 * N), BF16),
            jax.ShapeDtypeStruct((N, N), F32),
            jax.ShapeDtypeStruct((N, TILE_COLS), F32),
        ),
        in_specs=[vmem] * 3,
        out_specs=(anywhere,) + (vmem,) * 3,
        scratch_shapes=[pltpu.VMEM((N, LOCAL), F32), pltpu.SemaphoreType.DMA],
        compiler_params=pltpu.CompilerParams(vmem_limit_bytes=16 * MIB),
        cost_estimate=pl.CostEstimate(flops=1_000_000_000, bytes_accessed=0, transcendentals=0),
        name="near",
    )(near, inverse, trailing)
    left_factor, send = pl.pallas_call(
        far_kernel,
        out_shape=(
            jax.ShapeDtypeStruct((TILE_ROWS, 4 * N), BF16),
            jax.ShapeDtypeStruct((ROWS, 2 * N + PACKED, 128), F32),
        ),
        in_specs=[vmem] * 6 + [anywhere],
        out_specs=(vmem,) * 2,
        input_output_aliases={6: 0},
        compiler_params=pltpu.CompilerParams(vmem_limit_bytes=16 * MIB),
        name="far",
    )(far, inverse, rows, trailing, near_term, near_part, left_factor)
    recv = lax.all_to_all(send, "row", 0, 0, axis_index_groups=[ORDER])
    trailing_out, row_out, diag_out = pl.pallas_call(
        update_kernel,
        out_shape=(
            jax.ShapeDtypeStruct((TILE_ROWS, TILE_COLS), F32),
            jax.ShapeDtypeStruct((OWN, TILE_COLS), F32),
            jax.ShapeDtypeStruct((N, N), F32),
        ),
        in_specs=[vmem] * 7,
        out_specs=(anywhere,) * 3,
        scratch_shapes=[
            pltpu.VMEM((TILE_ROWS, TILE_COLS), F32),
            pltpu.VMEM((N, TILE_COLS), F32),
            pltpu.VMEM((4 * N, TILE_COLS), BF16),
            pltpu.VMEM((N, N), F32),
            pltpu.VMEM((OWN, TILE_COLS), F32),
            pltpu.VMEM((N, N), F32),
            pltpu.SemaphoreType.DMA((8,)),
            pltpu.SemaphoreType.DMA((2,)),
        ],
        compiler_params=pltpu.CompilerParams(vmem_limit_bytes=32 * MIB),
        name="update",
    )(recv, left_factor, inverse, diag_factor, diag_grad, row_grad, trailing_grad)
    return (panel_out, trailing_out, row_out, diag_out)


def solution(mesh):
    return jax.shard_map(
        per_device,
        mesh=mesh,
        in_specs=(
            P(None, ("row", "col")),
            P(None, ("row", "col")),
            P(),
            P(),
            P("row", "col"),
            P("row", "col"),
            P("row", "col"),
            P("row", "col"),
        ),
        out_specs=(P(None, ("row", "col")), P("row", "col"), P("row", "col"), P()),
        check_vma=False,
    )
```

```python
import functools

import jax
import jax.numpy as jnp
from jax import lax
from jax.experimental import pallas as pl
from jax.experimental.pallas import tpu as pltpu
from jax.sharding import PartitionSpec as P

N = 64
ROWS = 16
COLS = 8
LOCAL = 128
TILE_ROWS = COLS * LOCAL
TILE_COLS = 2048
OWN = N // ROWS
PIECES = TILE_COLS // 128
ORDER = [15, 14, 13, 12, 11, 10, 9, 8, 7, 6, 5, 4, 3, 2, 1, 0]
SLOT = [15, 14, 13, 12, 11, 10, 9, 8, 7, 6, 5, 4, 3, 2, 1, 0]
HIGHEST = lax.Precision.HIGHEST
F32 = jnp.float32
BF16 = jnp.bfloat16
MIB = 1024 * 1024


def dot(a, b, contract, precision=None):
    return lax.dot_general(
        a, b, ((contract[:1], contract[1:]), ((), ())), precision=precision, preferred_element_type=F32
    )


def split(value):
    high = value.astype(BF16)
    return high, (value - high.astype(F32)).astype(BF16)


def block_row(k, other):
    place = lax.axis_index("col")
    chip, core = place // 2, lax.rem(place, 2)
    core = 1 - core if other else core
    return pl.multiple_of((lax.rem(chip - k + 4, 4) * 2 + core) * LOCAL, LOCAL)


def prepare_kernel(
    payload_ref, factor_ref, row_panel_ref,
    inverse_ref, solver_ref, copy_ref, rows_ref,
):
    copy_ref[...] = payload_ref[...]
    factor = factor_ref[...]
    row = lax.broadcasted_iota(jnp.int32, (N, N), 0)
    col = lax.broadcasted_iota(jnp.int32, (N, N), 1)
    eye = jnp.where(row == col, 1.0, 0.0).astype(F32)
    diagonal = jnp.sum(factor * eye, axis=1, keepdims=True)
    diagonal_row = jnp.sum(factor * eye, axis=0, keepdims=True)
    below = jnp.where(row > col, factor, 0.0) / diagonal
    value = eye
    for j in range(N - 1):
        value = value - below[:, j : j + 1] * value[j : j + 1, :]
    inverse = value / diagonal_row
    inverse_ref[...] = inverse
    high, middle, low = thirds(inverse.T)
    solver_ref[...] = jnp.concatenate([high, high, high, middle, middle, low], axis=1)
    for j in range(PIECES):
        rows_ref[OWN * j : OWN * (j + 1), :] = row_panel_ref[:, 128 * j : 128 * (j + 1)]


def solve_line(line_ref, left_ref, first, solve):
    grads = jnp.concatenate([line_ref[k, :N, :] for k in range(4)], axis=1)
    panels = jnp.concatenate([line_ref[k, N:, :] for k in range(4)], axis=1)
    solved = solve(grads)
    high, low = split(solved)
    both = jnp.concatenate([high, low], axis=0)
    panel_high, panel_low = split(panels)
    term = dot(both, panel_high, (1, 1)) + dot(both, panel_low, (1, 1))
    doubled = jnp.concatenate([solved, solved], axis=0).T
    lane = lax.broadcasted_iota(jnp.int32, doubled.shape, 1)
    rounded = doubled.astype(BF16).astype(F32)
    pieces = jnp.where(lane < N, rounded, doubled - rounded).astype(BF16)
    part = slice(first, first + TILE_ROWS // 2)
    left_ref[part, : 2 * N] = pieces
    left_ref[part, 2 * N :] = pieces
    return solved, both, term[:N] + term[N:]


def line_product(both, tile_ref, cols, other):
    tile = jnp.concatenate([tile_ref[pl.ds(block_row(k, other), LOCAL), cols] for k in range(4)], axis=0)
    t_high, t_low = split(tile)
    part = dot(both, t_high, (1, 0)) + dot(both, t_low, (1, 0))
    return part[:N] + part[N:]


CHUNK = 256
HALF = N // 2
PACKED = 3 * HALF * HALF // 128


def thirds(value):
    high = value.astype(BF16)
    rest = value - high.astype(F32)
    middle = rest.astype(BF16)
    return high, middle, (rest - middle.astype(F32)).astype(BF16)


def solve_thirds(solver_ref, grads):
    high, middle, low = thirds(grads)
    return dot(solver_ref[...], jnp.concatenate([high, middle, low, high, middle, high], axis=0), (1, 0))


def pack_lower(term):
    blocks = jnp.concatenate([term[:HALF, :HALF], term[HALF:, :HALF], term[HALF:, HALF:]], axis=1)
    rest = jnp.concatenate([blocks[PACKED:, HALF * i : HALF * (i + 1)] for i in range(3)], axis=0)
    return jnp.concatenate([blocks[:PACKED], rest], axis=1)


def unpack_lower(packed):
    step = HALF - PACKED
    rest = jnp.concatenate([packed[step * i : step * (i + 1), 3 * HALF :] for i in range(3)], axis=1)
    blocks = jnp.concatenate([packed[:, : 3 * HALF], rest], axis=0)
    top = jnp.concatenate([blocks[:, :HALF], jnp.zeros((HALF, HALF), F32)], axis=1)
    return jnp.concatenate([top, blocks[:, HALF:]], axis=0)


def near_kernel(
    near_ref, inverse_ref, tile_ref,
    own_hbm, left_ref, term_ref, part_ref,
    own, sem,
):
    solved, both, term = solve_line(near_ref, left_ref, 0, lambda g: dot(inverse_ref[...], g, (0, 0), HIGHEST))
    own[...] = solved[:, :LOCAL]
    copy = pltpu.make_async_copy(own, own_hbm, sem)
    copy.start()
    term_ref[...] = term
    for i in range(TILE_COLS // CHUNK):
        cols = slice(i * CHUNK, (i + 1) * CHUNK)
        part_ref[:, cols] = line_product(both, tile_ref, cols, False)
    copy.wait()


def far_kernel(
    far_ref, solver_ref, rows_ref, tile_ref, near_term_ref, near_part_ref, near_left_ref,
    left_ref, send_ref,
):
    own_rows = rows_ref[...]
    for s in range(ROWS):
        send_ref[s, N : 2 * N, :] = own_rows
    _, both, term = solve_line(far_ref, left_ref, TILE_ROWS // 2, functools.partial(solve_thirds, solver_ref))
    term = term + near_term_ref[...]
    packed = pack_lower(term)
    for s in range(ROWS):
        send_ref[s, 2 * N :, :] = packed
    for i in range(TILE_COLS // CHUNK):
        cols = slice(i * CHUNK, (i + 1) * CHUNK)
        part = near_part_ref[:, cols] + line_product(both, tile_ref, cols, True)
        for s in range(ROWS):
            for jj in range(CHUNK // 128):
                j = i * (CHUNK // 128) + jj
                send_ref[SLOT[s], OWN * j : OWN * (j + 1), :] = part[OWN * s : OWN * (s + 1), 128 * jj : 128 * (jj + 1)]


def update_kernel(
    recv_ref, left, inverse_ref, factor_ref, diag_grad_ref, row_grad_ref, grad_ref,
    out_ref, row_out_hbm, diag_out_hbm,
    result, full, right, small, row_out, diag_out, out_sems, small_sems,
):
    stores = []
    edges = [0, 256, 512, 768, 1024, 1280, 1536, 1792, 2048]

    def step(i):
        cols = slice(edges[i], edges[i + 1])
        for s in range(ROWS):
            for j in range(edges[i] // 128, edges[i + 1] // 128):
                full[OWN * s : OWN * (s + 1), 128 * j : 128 * (j + 1)] = recv_ref[SLOT[s], N + OWN * j : N + OWN * (j + 1), :]
        high, low = split(full[:, cols])
        right[:, cols] = jnp.concatenate([high, high, low, low], axis=0)
        product = dot(left[...], right[:, cols], (1, 0))
        for slot in range(COLS):
            part = pl.ds(block_row(slot % 4, slot >= 4), LOCAL)
            result[part, cols] = grad_ref[part, cols] - product[slot * LOCAL : (slot + 1) * LOCAL]
        stores.append(pltpu.make_async_copy(result.at[:, cols], out_ref.at[:, cols], out_sems.at[i]))
        stores[-1].start()

    count = len(edges) - 1
    for i in range(4):
        step(i)

    packed = recv_ref[0, 2 * N :, :]
    reduced = recv_ref[0, :N, :]
    for s in range(1, ROWS):
        packed = packed + recv_ref[s, 2 * N :, :]
        reduced = reduced + recv_ref[s, :N, :]
    total = unpack_lower(packed)
    inverse, factor = inverse_ref[...], factor_ref[...]
    r_id = lax.broadcasted_iota(jnp.int32, (N, N), 0)
    c_id = lax.broadcasted_iota(jnp.int32, (N, N), 1)
    lower = r_id >= c_id
    dsum = diag_grad_ref[...] - jnp.where(lower, total, 0.0)
    phi = jnp.where(lower, dot(factor, dsum, (0, 0), HIGHEST), 0.0)
    phi = jnp.where(r_id == c_id, 0.5 * phi, phi)
    spart = dot(dot(inverse, phi, (0, 0), HIGHEST), inverse, (1, 0), HIGHEST)
    both = spart + spart.T
    diag_out[...] = 0.5 * both
    stores.append(pltpu.make_async_copy(diag_out, diag_out_hbm, small_sems.at[0]))
    stores[-1].start()
    small[...] = both
    own_both = small[pl.ds(lax.axis_index("row") * OWN, OWN), :]
    both_high, both_low = split(own_both)
    wide = jnp.concatenate([both_high, both_low, both_high, both_low], axis=1)

    for i in range(4, count):
        step(i)
    second = dot(wide, right[...], (1, 0))
    for j in range(PIECES):
        cols = slice(128 * j, 128 * (j + 1))
        row_out[:, cols] = row_grad_ref[:, cols] - reduced[OWN * j : OWN * (j + 1), :] - second[:, cols]
    stores.append(pltpu.make_async_copy(row_out, row_out_hbm, small_sems.at[1]))
    stores[-1].start()
    for copy in stores:
        copy.wait()


def across_chips(value, k):
    pairs = [(2 * x + c, 2 * ((x + k) % 4) + c) for x in range(4) for c in range(2)]
    return lax.ppermute(value, "col", pairs)


def per_device(panel_t, panel_grad_t, diag_factor, diag_grad, row_panel, row_grad, trailing, trailing_grad):
    vmem = pl.BlockSpec(memory_space=pltpu.VMEM)
    anywhere = pl.BlockSpec(memory_space=pl.ANY)
    payload = jnp.pad(panel_grad_t, ((0, N), (0, 0))) + jnp.pad(panel_t, ((N, 0), (0, 0)))
    opposite = across_chips(payload, 2)
    right = across_chips(payload, 1)
    left = across_chips(payload, 3)
    inverse, solver, payload, rows = pl.pallas_call(
        prepare_kernel,
        out_shape=(
            jax.ShapeDtypeStruct((N, N), F32),
            jax.ShapeDtypeStruct((N, 6 * N), BF16),
            jax.ShapeDtypeStruct((2 * N, LOCAL), F32),
            jax.ShapeDtypeStruct((N, 128), F32),
        ),
        in_specs=[vmem] * 3,
        out_specs=(vmem,) * 4,
        compiler_params=pltpu.CompilerParams(vmem_limit_bytes=4 * MIB),
        cost_estimate=pl.CostEstimate(flops=4_000_000_000, bytes_accessed=0, transcendentals=0),
        name="prepare",
    )(payload, diag_factor, row_panel)
    near = jnp.stack([payload, right, opposite, left])
    far = lax.ppermute(near, "col", [(i, i ^ 1) for i in range(COLS)])
    panel_out, left_factor, near_term, near_part = pl.pallas_call(
        near_kernel,
        out_shape=(
            jax.ShapeDtypeStruct((N, LOCAL), F32),
            jax.ShapeDtypeStruct((TILE_ROWS, 4 * N), BF16),
            jax.ShapeDtypeStruct((N, N), F32),
            jax.ShapeDtypeStruct((N, TILE_COLS), F32),
        ),
        in_specs=[vmem] * 3,
        out_specs=(anywhere,) + (vmem,) * 3,
        scratch_shapes=[pltpu.VMEM((N, LOCAL), F32), pltpu.SemaphoreType.DMA],
        compiler_params=pltpu.CompilerParams(vmem_limit_bytes=16 * MIB),
        cost_estimate=pl.CostEstimate(flops=1_000_000_000, bytes_accessed=0, transcendentals=0),
        name="near",
    )(near, inverse, trailing)
    left_factor, send = pl.pallas_call(
        far_kernel,
        out_shape=(
            jax.ShapeDtypeStruct((TILE_ROWS, 4 * N), BF16),
            jax.ShapeDtypeStruct((ROWS, 2 * N + PACKED, 128), F32),
        ),
        in_specs=[vmem] * 6 + [anywhere],
        out_specs=(vmem,) * 2,
        input_output_aliases={6: 0},
        compiler_params=pltpu.CompilerParams(vmem_limit_bytes=16 * MIB),
        name="far",
    )(far, solver, rows, trailing, near_term, near_part, left_factor)
    recv = lax.all_to_all(send, "row", 0, 0, axis_index_groups=[ORDER])
    trailing_out, row_out, diag_out = pl.pallas_call(
        update_kernel,
        out_shape=(
            jax.ShapeDtypeStruct((TILE_ROWS, TILE_COLS), F32),
            jax.ShapeDtypeStruct((OWN, TILE_COLS), F32),
            jax.ShapeDtypeStruct((N, N), F32),
        ),
        in_specs=[vmem] * 7,
        out_specs=(anywhere,) * 3,
        scratch_shapes=[
            pltpu.VMEM((TILE_ROWS, TILE_COLS), F32),
            pltpu.VMEM((N, TILE_COLS), F32),
            pltpu.VMEM((4 * N, TILE_COLS), BF16),
            pltpu.VMEM((N, N), F32),
            pltpu.VMEM((OWN, TILE_COLS), F32),
            pltpu.VMEM((N, N), F32),
            pltpu.SemaphoreType.DMA((8,)),
            pltpu.SemaphoreType.DMA((2,)),
        ],
        compiler_params=pltpu.CompilerParams(vmem_limit_bytes=32 * MIB),
        name="update",
    )(recv, left_factor, inverse, diag_factor, diag_grad, row_grad, trailing_grad)
    return (panel_out, trailing_out, row_out, diag_out)


def solution(mesh):
    return jax.shard_map(
        per_device,
        mesh=mesh,
        in_specs=(
            P(None, ("row", "col")),
            P(None, ("row", "col")),
            P(),
            P(),
            P("row", "col"),
            P("row", "col"),
            P("row", "col"),
            P("row", "col"),
        ),
        out_specs=(P(None, ("row", "col")), P("row", "col"), P("row", "col"), P()),
        check_vma=False,
    )
```

```python
import jax
import jax.numpy as jnp
from jax import lax
from jax.experimental import pallas as pl
from jax.experimental.pallas import tpu as pltpu
from jax.sharding import PartitionSpec as P

N = 64
ROWS = 16
COLS = 8
LOCAL = 128
TILE_ROWS = COLS * LOCAL
TILE_COLS = 2048
OWN = N // ROWS
PIECES = TILE_COLS // 128
ORDER = tuple(range(ROWS - 1, -1, -1))
HIGHEST = lax.Precision.HIGHEST
F32 = jnp.float32
BF16 = jnp.bfloat16
MIB = 1024 * 1024


def dot(a, b, contract, precision=None):
    return lax.dot_general(
        a, b, ((contract[:1], contract[1:]), ((), ())), precision=precision, preferred_element_type=F32
    )


def split(value):
    high = value.astype(BF16)
    return high, (value - high.astype(F32)).astype(BF16)


def block_row(k, other):
    place = lax.axis_index("col")
    chip, core = place // 2, lax.rem(place, 2)
    core = 1 - core if other else core
    return pl.multiple_of((lax.rem(chip - k + 4, 4) * 2 + core) * LOCAL, LOCAL)


def prepare_kernel(
    payload_ref, factor_ref,
    inverse_ref, copy_ref,
):
    copy_ref[...] = payload_ref[...]
    factor = factor_ref[...]
    row = lax.broadcasted_iota(jnp.int32, (N, N), 0)
    col = lax.broadcasted_iota(jnp.int32, (N, N), 1)
    eye = jnp.where(row == col, 1.0, 0.0).astype(F32)
    diagonal = jnp.sum(factor * eye, axis=1, keepdims=True)
    diagonal_row = jnp.sum(factor * eye, axis=0, keepdims=True)
    below = jnp.where(row > col, factor, 0.0) / diagonal
    value = eye
    for j in range(N - 1):
        value = value - below[:, j : j + 1] * value[j : j + 1, :]
    inverse_ref[...] = value / diagonal_row


def solve_line(line_ref, inverse_ref, left_ref, first):
    grads = jnp.concatenate([line_ref[k, :N, :] for k in range(4)], axis=1)
    panels = jnp.concatenate([line_ref[k, N:, :] for k in range(4)], axis=1)
    solved = dot(inverse_ref[...], grads, (0, 0), HIGHEST)
    high, low = split(solved)
    both = jnp.concatenate([high, low], axis=0)
    panel_high, panel_low = split(panels)
    term = dot(both, panel_high, (1, 1)) + dot(both, panel_low, (1, 1))
    doubled = jnp.concatenate([solved, solved], axis=0).T
    lane = lax.broadcasted_iota(jnp.int32, doubled.shape, 1)
    rounded = doubled.astype(BF16).astype(F32)
    pieces = jnp.where(lane < N, rounded, doubled - rounded).astype(BF16)
    part = slice(first, first + TILE_ROWS // 2)
    left_ref[part, : 2 * N] = pieces
    left_ref[part, 2 * N :] = pieces
    return solved, both, term[:N] + term[N:]


def line_product(both, tile_ref, cols, other):
    tile = jnp.concatenate([tile_ref[pl.ds(block_row(k, other), LOCAL), cols] for k in range(4)], axis=0)
    t_high, t_low = split(tile)
    part = dot(both, t_high, (1, 0)) + dot(both, t_low, (1, 0))
    return part[:N] + part[N:]


CHUNK = 256
HALF = N // 2
PACKED = 3 * HALF * HALF // 128


def pack_lower(term):
    blocks = jnp.concatenate([term[:HALF, :HALF], term[HALF:, :HALF], term[HALF:, HALF:]], axis=1)
    rest = jnp.concatenate([blocks[PACKED:, HALF * i : HALF * (i + 1)] for i in range(3)], axis=0)
    return jnp.concatenate([blocks[:PACKED], rest], axis=1)


def unpack_lower(packed):
    step = HALF - PACKED
    rest = jnp.concatenate([packed[step * i : step * (i + 1), 3 * HALF :] for i in range(3)], axis=1)
    blocks = jnp.concatenate([packed[:, : 3 * HALF], rest], axis=0)
    top = jnp.concatenate([blocks[:, :HALF], jnp.zeros((HALF, HALF), F32)], axis=1)
    return jnp.concatenate([top, blocks[:, HALF:]], axis=0)


def near_kernel(
    near_ref, inverse_ref, tile_ref,
    own_hbm, left_ref, term_ref, part_ref,
    own, sem,
):
    solved, both, term = solve_line(near_ref, inverse_ref, left_ref, 0)
    own[...] = solved[:, :LOCAL]
    copy = pltpu.make_async_copy(own, own_hbm, sem)
    copy.start()
    term_ref[...] = term
    for i in range(TILE_COLS // CHUNK):
        cols = slice(i * CHUNK, (i + 1) * CHUNK)
        part_ref[:, cols] = line_product(both, tile_ref, cols, False)
    copy.wait()


def far_kernel(
    far_ref, inverse_ref, tile_ref, near_term_ref, near_part_ref, near_left_ref,
    left_ref, send_hbm,
    send, sems,
):
    _, both, term = solve_line(far_ref, inverse_ref, left_ref, TILE_ROWS // 2)
    packed = pack_lower(term + near_term_ref[...])
    for s in range(ROWS):
        send[s, N:, :] = packed
    copies = [pltpu.make_async_copy(send.at[:, N:], send_hbm.at[:, N:], sems.at[0])]
    copies[0].start()
    height = OWN * CHUNK // 128
    for i in range(TILE_COLS // CHUNK):
        cols = slice(i * CHUNK, (i + 1) * CHUNK)
        part = near_part_ref[:, cols] + line_product(both, tile_ref, cols, True)
        for s in range(ROWS):
            for jj in range(CHUNK // 128):
                j = i * (CHUNK // 128) + jj
                send[ROWS - 1 - s, OWN * j : OWN * (j + 1), :] = part[OWN * s : OWN * (s + 1), 128 * jj : 128 * (jj + 1)]
        slots = pl.ds(i * height, height)
        copies.append(pltpu.make_async_copy(send.at[:, slots], send_hbm.at[:, slots], sems.at[i + 1]))
        copies[-1].start()
    for copy in copies:
        copy.wait()


def update_kernel(
    rows_ref, left, grad_ref,
    out_ref, right,
    result, out_sems,
):
    stores = []
    for i in range(TILE_COLS // CHUNK):
        cols = slice(i * CHUNK, (i + 1) * CHUNK)
        high, low = split(jnp.concatenate([rows_ref[ROWS - 1 - s, :, cols] for s in range(ROWS)], axis=0))
        right[:, cols] = jnp.concatenate([high, high, low, low], axis=0)
        product = dot(left[...], right[:, cols], (1, 0))
        for slot in range(COLS):
            part = pl.ds(block_row(slot % 4, slot >= 4), LOCAL)
            result[part, cols] = grad_ref[part, cols] - product[slot * LOCAL : (slot + 1) * LOCAL]
        stores.append(pltpu.make_async_copy(result.at[:, cols], out_ref.at[:, cols], out_sems.at[i]))
        stores[-1].start()
    for copy in stores:
        copy.wait()


def final_kernel(
    recv_ref, right, inverse_ref, factor_ref, diag_grad_ref, row_grad_ref,
    row_out_hbm, diag_out_hbm,
    small, row_out, diag_out, sems,
):
    packed = recv_ref[0, N:, :]
    reduced = recv_ref[0, :N, :]
    for s in range(1, ROWS):
        packed = packed + recv_ref[s, N:, :]
        reduced = reduced + recv_ref[s, :N, :]
    total = unpack_lower(packed)
    inverse, factor = inverse_ref[...], factor_ref[...]
    r_id = lax.broadcasted_iota(jnp.int32, (N, N), 0)
    c_id = lax.broadcasted_iota(jnp.int32, (N, N), 1)
    lower = r_id >= c_id
    dsum = diag_grad_ref[...] - jnp.where(lower, total, 0.0)
    phi = jnp.where(lower, dot(factor, dsum, (0, 0), HIGHEST), 0.0)
    phi = jnp.where(r_id == c_id, 0.5 * phi, phi)
    spart = dot(dot(inverse, phi, (0, 0), HIGHEST), inverse, (1, 0), HIGHEST)
    both = spart + spart.T
    diag_out[...] = 0.5 * both
    first = pltpu.make_async_copy(diag_out, diag_out_hbm, sems.at[0])
    first.start()
    small[...] = both
    own_both = small[pl.ds(lax.axis_index("row") * OWN, OWN), :]
    both_high, both_low = split(own_both)
    wide = jnp.concatenate([both_high, both_low, both_high, both_low], axis=1)
    second = dot(wide, right[...], (1, 0))
    for j in range(PIECES):
        cols = slice(128 * j, 128 * (j + 1))
        row_out[:, cols] = row_grad_ref[:, cols] - reduced[OWN * j : OWN * (j + 1), :] - second[:, cols]
    last = pltpu.make_async_copy(row_out, row_out_hbm, sems.at[1])
    last.start()
    first.wait()
    last.wait()


def across_chips(value, k):
    pairs = [(2 * x + c, 2 * ((x + k) % 4) + c) for x in range(4) for c in range(2)]
    return lax.ppermute(value, "col", pairs)


def per_device(panel_t, panel_grad_t, diag_factor, diag_grad, row_panel, row_grad, trailing, trailing_grad):
    vmem = pl.BlockSpec(memory_space=pltpu.VMEM)
    anywhere = pl.BlockSpec(memory_space=pl.ANY)
    payload = jnp.pad(panel_grad_t, ((0, N), (0, 0))) + jnp.pad(panel_t, ((N, 0), (0, 0)))
    opposite = across_chips(payload, 2)
    right = across_chips(payload, 1)
    left = across_chips(payload, 3)
    rows = lax.all_to_all(jnp.broadcast_to(row_panel[None], (ROWS, OWN, TILE_COLS)), "row", 0, 0, axis_index_groups=[ORDER])
    inverse, payload = pl.pallas_call(
        prepare_kernel,
        out_shape=(
            jax.ShapeDtypeStruct((N, N), F32),
            jax.ShapeDtypeStruct((2 * N, LOCAL), F32),
        ),
        in_specs=[vmem] * 2,
        out_specs=(vmem,) * 2,
        compiler_params=pltpu.CompilerParams(vmem_limit_bytes=4 * MIB),
        cost_estimate=pl.CostEstimate(flops=20000000000, bytes_accessed=0, transcendentals=0),
        name="prepare",
    )(payload, diag_factor)
    near = jnp.stack([payload, right, opposite, left])
    far = lax.ppermute(near, "col", [(i, i ^ 1) for i in range(COLS)])
    panel_out, left_factor, near_term, near_part = pl.pallas_call(
        near_kernel,
        out_shape=(
            jax.ShapeDtypeStruct((N, LOCAL), F32),
            jax.ShapeDtypeStruct((TILE_ROWS, 4 * N), BF16),
            jax.ShapeDtypeStruct((N, N), F32),
            jax.ShapeDtypeStruct((N, TILE_COLS), F32),
        ),
        in_specs=[vmem] * 3,
        out_specs=(anywhere,) + (vmem,) * 3,
        scratch_shapes=[pltpu.VMEM((N, LOCAL), F32), pltpu.SemaphoreType.DMA],
        compiler_params=pltpu.CompilerParams(vmem_limit_bytes=16 * MIB),
        cost_estimate=pl.CostEstimate(flops=4000000000, bytes_accessed=0, transcendentals=0),
        name="near",
    )(near, inverse, trailing)
    left_factor, send = pl.pallas_call(
        far_kernel,
        out_shape=(
            jax.ShapeDtypeStruct((TILE_ROWS, 4 * N), BF16),
            jax.ShapeDtypeStruct((ROWS, N + PACKED, 128), F32),
        ),
        in_specs=[vmem] * 5 + [anywhere],
        out_specs=(vmem, anywhere),
        scratch_shapes=[pltpu.VMEM((ROWS, N + PACKED, 128), F32), pltpu.SemaphoreType.DMA((9,))],
        input_output_aliases={5: 0},
        compiler_params=pltpu.CompilerParams(vmem_limit_bytes=20 * MIB),
        cost_estimate=pl.CostEstimate(flops=4_000_000_000, bytes_accessed=0, transcendentals=0),
        name="far",
    )(far, inverse, trailing, near_term, near_part, left_factor)
    recv = lax.all_to_all(send, "row", 0, 0, axis_index_groups=[ORDER])
    trailing_out, right_factor = pl.pallas_call(
        update_kernel,
        out_shape=(
            jax.ShapeDtypeStruct((TILE_ROWS, TILE_COLS), F32),
            jax.ShapeDtypeStruct((4 * N, TILE_COLS), BF16),
        ),
        in_specs=[vmem] * 3,
        out_specs=(anywhere, vmem),
        scratch_shapes=[pltpu.VMEM((TILE_ROWS, TILE_COLS), F32), pltpu.SemaphoreType.DMA((8,))],
        compiler_params=pltpu.CompilerParams(vmem_limit_bytes=32 * MIB),
        cost_estimate=pl.CostEstimate(flops=4_000_000_000, bytes_accessed=0, transcendentals=0),
        name="update",
    )(rows, left_factor, trailing_grad)
    row_out, diag_out = pl.pallas_call(
        final_kernel,
        out_shape=(
            jax.ShapeDtypeStruct((OWN, TILE_COLS), F32),
            jax.ShapeDtypeStruct((N, N), F32),
        ),
        in_specs=[vmem] * 6,
        out_specs=(anywhere,) * 2,
        scratch_shapes=[
            pltpu.VMEM((N, N), F32),
            pltpu.VMEM((OWN, TILE_COLS), F32),
            pltpu.VMEM((N, N), F32),
            pltpu.SemaphoreType.DMA((2,)),
        ],
        compiler_params=pltpu.CompilerParams(vmem_limit_bytes=8 * MIB),
        name="final",
    )(recv, right_factor, inverse, diag_factor, diag_grad, row_grad)
    return (panel_out, trailing_out, row_out, diag_out)


def solution(mesh):
    return jax.shard_map(
        per_device,
        mesh=mesh,
        in_specs=(
            P(None, ("row", "col")),
            P(None, ("row", "col")),
            P(),
            P(),
            P("row", "col"),
            P("row", "col"),
            P("row", "col"),
            P("row", "col"),
        ),
        out_specs=(P(None, ("row", "col")), P("row", "col"), P("row", "col"), P()),
        check_vma=False,
    )
```
